32 devices in a mesh: row: 4 (over z), col: 2 (over x), depth: 4 (over y, core).
Axes of the slice: x: 2, y: 2, z: 4, core: 2. Of those that a mesh axis runs over, the one named last changes fastest.
Arguments:
- grad_out: bfloat16 [2048, 3072], P(('row', 'depth'), 'col'), may hold values from -4 to 4
- input_stash: bfloat16 [2048, 3072], P(('row', 'depth'), 'col'), may hold values from -6 to 6
- input_scale: float32 [24, 2048], P('col', ('row', 'depth')), may hold values from 0.05 to 0.8
- hidden_stash: bfloat16 [2048, 12288], P(('row', 'depth'), 'col'), may hold values from -6 to 6
- hidden_scale: float32 [96, 2048], P('col', ('row', 'depth')), may hold values from 0.25 to 4
- first_weight: bfloat16 [3072, 12288], P('col', 'row'), may hold values from -0.0546875 to 0.0546875
- second_weight: bfloat16 [12288, 3072], P('col', 'row'), may hold values from -0.109375 to 0.109375
Outputs:
- input_grad: bfloat16 [2048, 3072], P(('row', 'depth'), 'col')
- first_grad: bfloat16 [3072, 12288], P('col', ('row', 'depth'))
- first_bias: float32 [12288], P(('row', 'depth'))
- second_grad: bfloat16 [12288, 3072], P('col', ('row', 'depth'))
- second_bias: float32 [3072], P(('row', 'depth'))
The draws below stay inside these ranges and needn't reach their ends.
All inputs are finite; a program needn't handle non-finite values.
Results may differ from the reference program's by a relative error of at most 0.015.
Values may be sent and summed in bfloat16 or wider, within the bound.
No kernel may reach another device: no remote copies, remote signals or barrier semaphores. Data moves between devices by JAX's collectives and lax.ppermute only.
A program may use at most 192 MiB of HBM per device.

```python
import math
import jax
import jax.numpy as jnp
from jax import lax

D = 3072
FF = 12288
QBLOCK = 128
TOK_DEV = 128
TOKENS = 2048
SLICES = 4


def block_scale(rng, shape, cuts, low, largest):
    loudness = 1.0
    for dim, parts in cuts:
        draws = jax.random.uniform(jax.random.fold_in(jax.random.fold_in(rng, 6), dim), (parts,), jnp.float32, low / len(cuts), largest / len(cuts))
        loudness = loudness * jnp.repeat(jnp.exp(draws), shape[dim] // parts).reshape((-1,) + (1,) * (len(shape) - 1 - dim))
    return loudness


def scatter_about(key, dims, deviation, reach, split=(), held_as=jnp.bfloat16):
    loudness = block_scale(key, dims, split, -0.22, 0.18) if split else 1.0
    drawn = jax.random.normal(key, dims, jnp.float32) * deviation * loudness
    return jnp.minimum(jnp.maximum(drawn, -reach), reach).astype(held_as)


def setup_inputs(seed: int = 0) -> dict:
    key_list = jax.random.split(jax.random.key(seed), 8)
    return {
        "grad_out": scatter_about(key_list[0], (TOKENS, D), 0.5, 4.0, ((0, 16), (1, 2))),
        "input_stash": scatter_about(key_list[1], (TOKENS, D), 1.0, 6.0, ((0, 16), (1, 2))),
        "input_scale": jnp.clip(jnp.exp(math.log(0.8) - 2.7725887 * jax.random.uniform(key_list[2], (D // QBLOCK, TOKENS), jnp.float32) ** block_scale(key_list[2], (D // QBLOCK, TOKENS), ((0, 2), (1, 16)), -0.2, 0.2)), 0.05, 0.8),
        "hidden_stash": scatter_about(key_list[3], (TOKENS, FF), 1.0, 6.0, ((0, 16), (1, 2))),
        "hidden_scale": jnp.clip(jnp.exp(math.log(4.0) - 2.7725887 * jax.random.uniform(key_list[4], (FF // QBLOCK, TOKENS), jnp.float32) ** block_scale(key_list[4], (FF // QBLOCK, TOKENS), ((0, 2), (1, 16)), -0.2, 0.2)), 0.25, 4.0),
        "first_weight": scatter_about(key_list[5], (D, FF), FF ** -0.5, 0.0546875, ((0, 2), (1, 4))),
        "second_weight": scatter_about(key_list[6], (FF, D), D ** -0.5, 0.109375, ((0, 2), (1, 4))),
    }


root_two_over_pi = 0.7978845608028654
cubic_coef = 0.044715
contract_last = (((1,), (1,)), ((), ()))


def dequantize(values, scales):
    height = values.shape[0]
    breadth = values.shape[1]
    blocks = values.astype(jnp.float32).reshape(height, breadth // QBLOCK, QBLOCK)
    return (blocks * jnp.transpose(scales)[:, :, None]).reshape(height, breadth)


def gelu_value(before):
    tangent = jnp.tanh(root_two_over_pi * (before + cubic_coef * before * before * before))
    return 0.5 * before * (1.0 + tangent)


def gelu_slope(before):
    tangent = jnp.tanh(root_two_over_pi * (before + cubic_coef * before * before * before))
    return 0.5 * (1.0 + tangent) + 0.5 * before * (1.0 - tangent * tangent) * root_two_over_pi * (1.0 + 3.0 * cubic_coef * before * before)


def by_slice(array):
    breadth = array.shape[1]
    grouped = array.reshape(TOKENS // (SLICES * TOK_DEV), SLICES, TOK_DEV, breadth)
    return jnp.transpose(grouped, (1, 0, 2, 3)).reshape(SLICES, TOKENS // SLICES, breadth)


def rounded(value):
    return lax.optimization_barrier(value.astype(jnp.bfloat16)).astype(jnp.float32)


def reference(grad_out, input_stash, input_scale, hidden_stash, hidden_scale, first_weight, second_weight):
    inputs = dequantize(input_stash, input_scale).astype(jnp.bfloat16)
    before_gelu = dequantize(hidden_stash, hidden_scale)
    hidden = gelu_value(before_gelu).astype(jnp.bfloat16)
    hidden_grad = lax.dot_general(grad_out, second_weight, contract_last, preferred_element_type=jnp.float32)
    gelu_grad = (hidden_grad * gelu_slope(before_gelu)).astype(jnp.bfloat16)
    input_grad = lax.dot_general(gelu_grad, first_weight, contract_last, preferred_element_type=jnp.float32).astype(jnp.bfloat16)

    def accumulate(totals, pieces):
        input_part, gelu_part, hidden_part, output_part = pieces
        first_total = totals[0] + rounded(jnp.dot(input_part.T, gelu_part, preferred_element_type=jnp.float32))
        first_sum = totals[1] + rounded(jnp.sum(gelu_part.astype(jnp.float32), axis=0))
        second_total = totals[2] + rounded(jnp.dot(hidden_part.T, output_part, preferred_element_type=jnp.float32))
        second_sum = totals[3] + rounded(jnp.sum(output_part.astype(jnp.float32), axis=0))
        return (first_total, first_sum, second_total, second_sum), None

    start = (jnp.zeros((D, FF), jnp.float32), jnp.zeros((FF,), jnp.float32), jnp.zeros((FF, D), jnp.float32), jnp.zeros((D,), jnp.float32))
    totals, _ = lax.scan(accumulate, start, (by_slice(inputs), by_slice(gelu_grad), by_slice(hidden), by_slice(grad_out)))
    return (input_grad, totals[0].astype(jnp.bfloat16), totals[1], totals[2].astype(jnp.bfloat16), totals[3])
```

```python
import jax
import jax.numpy as jnp
from jax import lax
from jax.sharding import PartitionSpec as P

root_two_over_pi = 0.7978845608028654
cubic_coef = 0.044715
contract_last = (((1,), (1,)), ((), ()))
contract_first = (((0,), (0,)), ((), ()))


def dequantize(values, scales):
    height = values.shape[0]
    breadth = values.shape[1]
    block = breadth // scales.shape[0]
    blocks = values.astype(jnp.float32).reshape(height, breadth // block, block)
    return (blocks * jnp.transpose(scales)[:, :, None]).reshape(height, breadth)


def gelu_value(before):
    tangent = jnp.tanh(root_two_over_pi * (before + cubic_coef * before * before * before))
    return 0.5 * before * (1.0 + tangent)


def gelu_slope(before):
    tangent = jnp.tanh(root_two_over_pi * (before + cubic_coef * before * before * before))
    return 0.5 * (1.0 + tangent) + 0.5 * before * (1.0 - tangent * tangent) * root_two_over_pi * (
        1.0 + 3.0 * cubic_coef * before * before
    )


def per_device(
    grad_out, input_stash, input_scale, hidden_stash, hidden_scale, first_weight, second_weight
):
    full_grad = lax.all_gather(grad_out, "col", axis=1, tiled=True)
    grad_rows = lax.all_to_all(full_grad, "row", split_axis=1, concat_axis=0, tiled=True)
    hidden_part = lax.dot_general(
        grad_rows, second_weight, contract_last, preferred_element_type=jnp.float32
    ).astype(jnp.bfloat16)
    hidden_grad = lax.psum_scatter(hidden_part, "row", scatter_dimension=0, tiled=True).astype(
        jnp.float32
    )
    before_gelu = dequantize(hidden_stash, hidden_scale)
    hidden_own = gelu_value(before_gelu).astype(jnp.bfloat16)
    gelu_grad = (hidden_grad * gelu_slope(before_gelu)).astype(jnp.bfloat16)
    full_gelu = lax.all_gather(gelu_grad, "col", axis=1, tiled=True)
    gelu_rows = lax.all_to_all(full_gelu, "row", split_axis=1, concat_axis=0, tiled=True)
    input_part = lax.dot_general(
        gelu_rows, first_weight, contract_last, preferred_element_type=jnp.float32
    ).astype(jnp.bfloat16)
    input_grad = lax.psum_scatter(input_part, "row", scatter_dimension=0, tiled=True)
    inputs_own = dequantize(input_stash, input_scale).astype(jnp.bfloat16)
    inputs = lax.all_gather(inputs_own, "row", axis=0, tiled=True)
    hidden = lax.all_gather(hidden_own, "row", axis=0, tiled=True)
    first_term = lax.dot_general(
        inputs, gelu_rows, contract_first, preferred_element_type=jnp.float32
    )
    first_column = jnp.sum(gelu_rows.astype(jnp.float32), axis=0)
    second_term = lax.dot_general(
        hidden, grad_rows, contract_first, preferred_element_type=jnp.float32
    )
    second_column = jnp.sum(grad_rows.astype(jnp.float32), axis=0)
    first_grad = lax.psum_scatter(
        first_term.astype(jnp.bfloat16), "depth", scatter_dimension=1, tiled=True
    )
    first_bias = lax.psum_scatter(
        first_column.astype(jnp.bfloat16), "depth", scatter_dimension=0, tiled=True
    ).astype(jnp.float32)
    second_grad = lax.psum_scatter(
        second_term.astype(jnp.bfloat16), "depth", scatter_dimension=1, tiled=True
    )
    second_bias = lax.psum_scatter(
        second_column.astype(jnp.bfloat16), "depth", scatter_dimension=0, tiled=True
    ).astype(jnp.float32)
    return input_grad, first_grad, first_bias, second_grad, second_bias


def solution(mesh):
    placed = (
        P(("row", "depth"), "col"),
        P(("row", "depth"), "col"),
        P("col", ("row", "depth")),
        P(("row", "depth"), "col"),
        P("col", ("row", "depth")),
        P("col", "row"),
        P("col", "row"),
    )
    return jax.shard_map(
        per_device,
        mesh=mesh,
        in_specs=placed,
        out_specs=(
            P(("row", "depth"), "col"),
            P("col", ("row", "depth")),
            P(("row", "depth")),
            P("col", ("row", "depth")),
            P(("row", "depth")),
        ),
        check_vma=False,
    )
```

```python
import jax
import jax.numpy as jnp
from jax import lax
from jax.experimental import pallas as pl
from jax.experimental.pallas import tpu as pltpu
from jax.sharding import PartitionSpec as P

root_two_over_pi = 0.7978845608028654
cubic_coef = 0.044715
contract_last = (((1,), (1,)), ((), ()))
contract_first = (((0,), (0,)), ((), ()))


def dequantize(values, scales):
    height = values.shape[0]
    breadth = values.shape[1]
    block = breadth // scales.shape[0]
    blocks = values.astype(jnp.float32).reshape(height, breadth // block, block)
    return (blocks * jnp.transpose(scales)[:, :, None]).reshape(height, breadth)


def gelu_value(before):
    tangent = jnp.tanh(root_two_over_pi * (before + cubic_coef * before * before * before))
    return 0.5 * before * (1.0 + tangent)


def gelu_slope(before):
    tangent = jnp.tanh(root_two_over_pi * (before + cubic_coef * before * before * before))
    return 0.5 * (1.0 + tangent) + 0.5 * before * (1.0 - tangent * tangent) * root_two_over_pi * (
        1.0 + 3.0 * cubic_coef * before * before
    )


def per_device_general(
    grad_out, input_stash, input_scale, hidden_stash, hidden_scale, first_weight, second_weight
):
    full_grad = lax.all_gather(grad_out, "col", axis=1, tiled=True)
    grad_rows = lax.all_to_all(full_grad, "row", split_axis=1, concat_axis=0, tiled=True)
    hidden_part = lax.dot_general(
        grad_rows, second_weight, contract_last, preferred_element_type=jnp.float32
    ).astype(jnp.bfloat16)
    hidden_grad = lax.psum_scatter(hidden_part, "row", scatter_dimension=0, tiled=True).astype(
        jnp.float32
    )
    before_gelu = dequantize(hidden_stash, hidden_scale)
    hidden_own = gelu_value(before_gelu).astype(jnp.bfloat16)
    gelu_grad = (hidden_grad * gelu_slope(before_gelu)).astype(jnp.bfloat16)
    full_gelu = lax.all_gather(gelu_grad, "col", axis=1, tiled=True)
    gelu_rows = lax.all_to_all(full_gelu, "row", split_axis=1, concat_axis=0, tiled=True)
    input_part = lax.dot_general(
        gelu_rows, first_weight, contract_last, preferred_element_type=jnp.float32
    ).astype(jnp.bfloat16)
    input_grad = lax.psum_scatter(input_part, "row", scatter_dimension=0, tiled=True)
    inputs_own = dequantize(input_stash, input_scale).astype(jnp.bfloat16)
    inputs = lax.all_gather(inputs_own, "row", axis=0, tiled=True)
    hidden = lax.all_gather(hidden_own, "row", axis=0, tiled=True)
    first_term = lax.dot_general(
        inputs, gelu_rows, contract_first, preferred_element_type=jnp.float32
    )
    first_column = jnp.sum(gelu_rows.astype(jnp.float32), axis=0)
    second_term = lax.dot_general(
        hidden, grad_rows, contract_first, preferred_element_type=jnp.float32
    )
    second_column = jnp.sum(grad_rows.astype(jnp.float32), axis=0)
    first_grad = lax.psum_scatter(
        first_term.astype(jnp.bfloat16), "depth", scatter_dimension=1, tiled=True
    )
    first_bias = lax.psum_scatter(
        first_column.astype(jnp.bfloat16), "depth", scatter_dimension=0, tiled=True
    ).astype(jnp.float32)
    second_grad = lax.psum_scatter(
        second_term.astype(jnp.bfloat16), "depth", scatter_dimension=1, tiled=True
    )
    second_bias = lax.psum_scatter(
        second_column.astype(jnp.bfloat16), "depth", scatter_dimension=0, tiled=True
    ).astype(jnp.float32)
    return input_grad, first_grad, first_bias, second_grad, second_bias


CHUNKS = 2


def dot(left, right, dims):
    return lax.dot_general(left, right, dims, preferred_element_type=jnp.float32)


def narrow(value):
    return value.astype(jnp.bfloat16)


def wide(value):
    return value.astype(jnp.float32)


def pick(array, index):
    return lax.dynamic_index_in_dim(array, index, 0, keepdims=False)


def columns(array, start, size):
    return lax.dynamic_slice_in_dim(array, start, size, 1)


def over_depth(value, bits):
    return lax.ppermute(value, "depth", [(i, i ^ bits) for i in range(4)])


def over_row(value, bits):
    return lax.ppermute(value, "row", [(i, i ^ bits) for i in range(4)])


def over_col(value):
    return lax.ppermute(value, "col", [(0, 1), (1, 0)])


def row_ends_in(value):
    return lax.ppermute(value, "row", [(0, 1), (3, 2)])


def row_mids_swap(value):
    return lax.ppermute(value, "row", [(1, 2), (2, 1)])


def row_mids_out(value):
    return lax.ppermute(value, "row", [(1, 0), (2, 3)])


def is_mid():
    row = lax.axis_index("row")
    return (row == 1) | (row == 2)


def row_gather(value):
    near = jnp.concatenate([value, over_row(value, 1)])
    across = row_mids_swap(near)
    return near, jnp.where(is_mid(), across, row_mids_out(across))


def after(value, *others):
    return lax.optimization_barrier((value,) + others)[0]


def row_scatter(others, partner, own, taken):
    across = row_mids_swap(narrow(others() + wide(taken)))
    size = across.shape[0] // 2
    beside = over_row(narrow(partner() + wide(across[size:])), 1)
    return (lambda: own() + wide(across[:size]) + wide(beside)), across, beside


def depth_start(partial):
    depth = lax.axis_index("depth")
    far = over_depth(narrow(partial(depth ^ 3)), 1)
    near = over_depth(narrow(partial(depth ^ 1)), 1)
    across = over_depth(narrow(partial(depth ^ 2) + wide(far)), 2)
    return near, across


def depth_end(partial, arrived):
    near, across = arrived
    return partial(lax.axis_index("depth")) + wide(near) + wide(across)


def spread_grad(grad_out):
    row, col = lax.axis_index("row"), lax.axis_index("col")
    breadth = grad_out.shape[1] // 2
    pieces = []
    for step in range(4):
        pairs = [
            (((2 * (r % 2) + c) ^ step) * 2 + r // 2, r * 2 + c) for r in range(4) for c in range(2)
        ]
        second = ((row ^ step) >> 1) & 1
        part = columns(grad_out, second * breadth, breadth)
        pieces.append(lax.ppermute(part, ("row", "col"), pairs))
    stacked = jnp.stack(pieces)
    base = 2 * (row & 1) + col
    order = [row, row ^ 1, jnp.where(row < 2, 2, 1), jnp.where(row < 2, 3, 0)]
    return jnp.concatenate([pick(stacked, base ^ r) for r in order])


def spread_gelu(gelu):
    row, col = lax.axis_index("row"), lax.axis_index("col")
    half = gelu.shape[0] // 2
    units = gelu.shape[1] // 2
    other = over_col(lax.dynamic_slice_in_dim(gelu, (1 - col) * half, half, 0))
    own = lax.dynamic_slice_in_dim(gelu, col * half, half, 0)
    here = (row >> 1) == col
    pieces = []
    for bits in (3, 2, 1, 0):
        source = jnp.where(here == (bits < 2), own, other)
        piece = columns(source, ((row ^ bits) & 1) * units, units)
        pieces.insert(0, over_row(piece, bits) if bits else piece)
    mine = jnp.concatenate(pieces)
    return jnp.concatenate([mine, over_col(mine)])


def hidden_kernel(stash, scale, *outs):
    halves, slopes = outs[:2], outs[2:]
    blocks = scale.shape[1]
    width = stash.shape[1] // blocks
    for b in range(blocks):
        before = stash[:, b * width : (b + 1) * width].astype(jnp.float32) * scale[:, b : b + 1]
        square = before * before
        tangent = jnp.tanh(root_two_over_pi * (before + cubic_coef * square * before))
        rise = 0.5 * (1.0 + tangent)
        value = before * rise
        slope = rise + 0.5 * before * (1.0 - tangent * tangent) * root_two_over_pi * (
            1.0 + 3.0 * cubic_coef * square
        )
        half, place = divmod(b, blocks // 2)
        halves[half][:, place * width : (place + 1) * width] = value.astype(jnp.bfloat16)
        group, inside = divmod(b, blocks // 8)
        chunk, inside = divmod(inside, blocks // (8 * CHUNKS))
        place = group * (blocks // (8 * CHUNKS)) + inside
        slopes[chunk][:, place * width : (place + 1) * width] = slope


def inputs_kernel(stash, scale, out):
    blocks = scale.shape[1]
    width = stash.shape[1] // blocks
    for b in range(blocks):
        part = slice(b * width, (b + 1) * width)
        out[:, part] = (stash[:, part].astype(jnp.float32) * scale[:, b : b + 1]).astype(jnp.bfloat16)


def elementwise(kernel, shapes, *operands):
    return pl.pallas_call(
        kernel,
        out_shape=shapes,
        compiler_params=pltpu.CompilerParams(vmem_limit_bytes=40 * 2**20),
        cost_estimate=pl.CostEstimate(
            flops=20 * operands[0].size,
            bytes_accessed=8 * operands[0].size,
            transcendentals=operands[0].size,
        ),
    )(*operands)


def chunk_rows(array, chunk):
    cut = array.reshape((8, CHUNKS, array.shape[0] // (8 * CHUNKS)) + array.shape[1:])
    return lax.index_in_dim(cut, chunk, 1, keepdims=False).reshape((-1,) + array.shape[1:])


def per_device_fast(
    grad_out, input_stash, input_scale, hidden_stash, hidden_scale, first_weight, second_weight
):
    col = lax.axis_index("col")
    mid = is_mid()
    tokens, units = hidden_stash.shape
    half = tokens // 2
    piece = units // (8 * CHUNKS)

    grad_rows = spread_grad(grad_out)
    share = grad_rows.shape[1] // 4

    struct = jax.ShapeDtypeStruct
    local = elementwise(
        hidden_kernel,
        [struct((tokens, units // 2), jnp.bfloat16)] * 2
        + [struct((tokens, units // CHUNKS), jnp.float32)] * CHUNKS,
        hidden_stash,
        jnp.transpose(hidden_scale),
    )
    hidden_own, slopes = local[:2], local[2:]
    inputs_own = elementwise(
        inputs_kernel,
        struct(input_stash.shape, jnp.bfloat16),
        input_stash,
        jnp.transpose(input_scale),
    )

    weights = [chunk_rows(second_weight, chunk) for chunk in range(CHUNKS)]
    grad_own, grad_partner = grad_rows[:tokens], grad_rows[tokens : 2 * tokens]
    grad_near, grad_others = grad_rows[: 2 * tokens], grad_rows[2 * tokens :]

    def terms(weight):
        return (
            lambda: dot(grad_others, weight, contract_last),
            lambda: dot(grad_partner, weight, contract_last),
            lambda: dot(grad_own, weight, contract_last),
        )

    def second_term(near, others):
        def partial(d):
            return dot(near, columns(grad_near, d * share, share), contract_first) + dot(
                others, columns(grad_others, d * share, share), contract_first
            )

        return partial

    takens, ends, acrosses, besides = [], [], [], []
    for chunk in range(CHUNKS):
        others, partner, own = terms(weights[chunk])
        sent = narrow(others())
        if chunk:
            sent = after(sent, takens[-1])
        takens.append(row_ends_in(sent))
        end, across, beside = row_scatter(others, partner, own, takens[-1])
        ends.append(end)
        acrosses.append(across)
        besides.append(beside)

    parts = [second_term(*row_gather(hidden_own[0]))]
    arrived = [depth_start(parts[0])]
    inputs_near, inputs_others = row_gather(after(inputs_own, takens[0]))
    third, fourth = inputs_others[:tokens], inputs_others[tokens:]
    by_row = [
        inputs_near[:tokens],
        inputs_near[tokens:],
        jnp.where(mid, fourth, third),
        jnp.where(mid, third, fourth),
    ]
    inputs = jnp.concatenate(
        [jnp.where(col == 0, r[:half], r[half:]) for r in by_row]
        + [jnp.where(col == 0, r[half:], r[:half]) for r in by_row]
    )
    parts.append(second_term(*row_gather(after(hidden_own[1], acrosses[0]))))

    gelus, firsts = [], []

    def first_term(gelu_rows):
        return lambda d: dot(inputs, columns(gelu_rows, d * piece, piece), contract_first)

    for chunk in range(CHUNKS):
        gelu_rows = spread_gelu(narrow(ends[chunk]() * slopes[chunk]))
        gelus.append(gelu_rows)
        firsts.append(depth_start(first_term(gelu_rows)))
    arrived.append(depth_start(parts[1]))

    gelu_rows = jnp.concatenate(
        [g[:, d * piece : (d + 1) * piece] for d in range(4) for g in gelus], axis=1
    )
    cut = gelu_rows.reshape(2, 4, half, units // 2)
    near = jnp.where(mid, cut[:, 3], cut[:, 2]).reshape(tokens, -1)
    end = jnp.where(mid, cut[:, 2], cut[:, 3]).reshape(tokens, -1)
    pair = jnp.concatenate([near, end])

    def others():
        return dot(pair, first_weight, contract_last)

    end, _, _ = row_scatter(
        others,
        lambda: dot(cut[:, 1].reshape(tokens, -1), first_weight, contract_last),
        lambda: dot(cut[:, 0].reshape(tokens, -1), first_weight, contract_last),
        row_ends_in(narrow(others())),
    )
    input_grad = narrow(end())
    front, back = input_grad[:half], input_grad[half:]
    input_grad = jnp.concatenate(
        [jnp.where(col == 0, front, back), jnp.where(col == 0, back, front)]
    )

    second_grad = jnp.concatenate([narrow(depth_end(p, a)) for p, a in zip(parts, arrived)])
    first_grad = jnp.concatenate(
        [narrow(depth_end(first_term(g), a)) for g, a in zip(gelus, firsts)], axis=1
    )

    def bias(array):
        sums = jnp.sum(wide(array), axis=0).reshape(4, -1)
        return depth_end(lambda d: pick(sums, d), depth_start(lambda d: pick(sums, d)))

    return input_grad, first_grad, bias(gelu_rows), second_grad, bias(grad_rows)


def solution(mesh):
    placed = (
        P(("row", "depth"), "col"),
        P(("row", "depth"), "col"),
        P("col", ("row", "depth")),
        P(("row", "depth"), "col"),
        P("col", ("row", "depth")),
        P("col", "row"),
        P("col", "row"),
    )
    sizes = dict(mesh.shape)
    fast = sizes["row"] == 4 and sizes["col"] == 2 and sizes["depth"] == 4
    return jax.shard_map(
        per_device_fast if fast else per_device_general,
        mesh=mesh,
        in_specs=placed,
        out_specs=(
            P(("row", "depth"), "col"),
            P("col", ("row", "depth")),
            P(("row", "depth")),
            P("col", ("row", "depth")),
            P(("row", "depth")),
        ),
        check_vma=False,
    )
```

```python
import jax
import jax.numpy as jnp
from jax import lax
from jax.experimental import pallas as pl
from jax.experimental.pallas import tpu as pltpu
from jax.sharding import PartitionSpec as P

root_two_over_pi = 0.7978845608028654
cubic_coef = 0.044715
contract_last = (((1,), (1,)), ((), ()))
contract_first = (((0,), (0,)), ((), ()))


def dequantize(values, scales):
    height = values.shape[0]
    breadth = values.shape[1]
    block = breadth // scales.shape[0]
    blocks = values.astype(jnp.float32).reshape(height, breadth // block, block)
    return (blocks * jnp.transpose(scales)[:, :, None]).reshape(height, breadth)


def gelu_value(before):
    tangent = jnp.tanh(root_two_over_pi * (before + cubic_coef * before * before * before))
    return 0.5 * before * (1.0 + tangent)


def gelu_slope(before):
    tangent = jnp.tanh(root_two_over_pi * (before + cubic_coef * before * before * before))
    return 0.5 * (1.0 + tangent) + 0.5 * before * (1.0 - tangent * tangent) * root_two_over_pi * (
        1.0 + 3.0 * cubic_coef * before * before
    )


def per_device_general(
    grad_out, input_stash, input_scale, hidden_stash, hidden_scale, first_weight, second_weight
):
    full_grad = lax.all_gather(grad_out, "col", axis=1, tiled=True)
    grad_rows = lax.all_to_all(full_grad, "row", split_axis=1, concat_axis=0, tiled=True)
    hidden_part = lax.dot_general(
        grad_rows, second_weight, contract_last, preferred_element_type=jnp.float32
    ).astype(jnp.bfloat16)
    hidden_grad = lax.psum_scatter(hidden_part, "row", scatter_dimension=0, tiled=True).astype(
        jnp.float32
    )
    before_gelu = dequantize(hidden_stash, hidden_scale)
    hidden_own = gelu_value(before_gelu).astype(jnp.bfloat16)
    gelu_grad = (hidden_grad * gelu_slope(before_gelu)).astype(jnp.bfloat16)
    full_gelu = lax.all_gather(gelu_grad, "col", axis=1, tiled=True)
    gelu_rows = lax.all_to_all(full_gelu, "row", split_axis=1, concat_axis=0, tiled=True)
    input_part = lax.dot_general(
        gelu_rows, first_weight, contract_last, preferred_element_type=jnp.float32
    ).astype(jnp.bfloat16)
    input_grad = lax.psum_scatter(input_part, "row", scatter_dimension=0, tiled=True)
    inputs_own = dequantize(input_stash, input_scale).astype(jnp.bfloat16)
    inputs = lax.all_gather(inputs_own, "row", axis=0, tiled=True)
    hidden = lax.all_gather(hidden_own, "row", axis=0, tiled=True)
    first_term = lax.dot_general(
        inputs, gelu_rows, contract_first, preferred_element_type=jnp.float32
    )
    first_column = jnp.sum(gelu_rows.astype(jnp.float32), axis=0)
    second_term = lax.dot_general(
        hidden, grad_rows, contract_first, preferred_element_type=jnp.float32
    )
    second_column = jnp.sum(grad_rows.astype(jnp.float32), axis=0)
    first_grad = lax.psum_scatter(
        first_term.astype(jnp.bfloat16), "depth", scatter_dimension=1, tiled=True
    )
    first_bias = lax.psum_scatter(
        first_column.astype(jnp.bfloat16), "depth", scatter_dimension=0, tiled=True
    ).astype(jnp.float32)
    second_grad = lax.psum_scatter(
        second_term.astype(jnp.bfloat16), "depth", scatter_dimension=1, tiled=True
    )
    second_bias = lax.psum_scatter(
        second_column.astype(jnp.bfloat16), "depth", scatter_dimension=0, tiled=True
    ).astype(jnp.float32)
    return input_grad, first_grad, first_bias, second_grad, second_bias


CHUNKS = 2


def dot(left, right, dims):
    return lax.dot_general(left, right, dims, preferred_element_type=jnp.float32)


def narrow(value):
    return value.astype(jnp.bfloat16)


def wide(value):
    return value.astype(jnp.float32)


def pick(array, index):
    return lax.dynamic_index_in_dim(array, index, 0, keepdims=False)


def columns(array, start, size):
    return lax.dynamic_slice_in_dim(array, start, size, 1)


def over_depth(value, bits):
    return lax.ppermute(value, "depth", [(i, i ^ bits) for i in range(4)])


def over_row(value, bits):
    return lax.ppermute(value, "row", [(i, i ^ bits) for i in range(4)])


def over_col(value):
    return lax.ppermute(value, "col", [(0, 1), (1, 0)])


def row_ends_in(value):
    return lax.ppermute(value, "row", [(0, 1), (3, 2)])


def row_mids_swap(value):
    return lax.ppermute(value, "row", [(1, 2), (2, 1)])


def row_mids_out(value):
    return lax.ppermute(value, "row", [(1, 0), (2, 3)])


def is_mid():
    row = lax.axis_index("row")
    return (row == 1) | (row == 2)


def after(value, *others):
    return lax.optimization_barrier((value,) + others)[0]


def row_gather(value, *waits):
    near = jnp.concatenate([value, over_row(value, 1)])
    across = row_mids_swap(after(near, *waits))
    return near, jnp.where(is_mid(), across, row_mids_out(across)), across


def row_scatter(others, partner, own, taken):
    across = row_mids_swap(narrow(others() + wide(taken)))
    size = across.shape[0] // 2
    beside = over_row(narrow(partner() + wide(across[size:])), 1)
    return (lambda: own() + wide(across[:size]) + wide(beside)), across, beside


def depth_start(partial):
    depth = lax.axis_index("depth")
    far = over_depth(narrow(partial(depth ^ 3)), 1)
    near = over_depth(narrow(partial(depth ^ 1)), 1)
    sent = narrow(partial(depth ^ 2) + wide(far))
    return near, over_depth(sent, 2), sent


def depth_end(partial, arrived):
    near, across, _ = arrived
    return partial(lax.axis_index("depth")) + wide(near) + wide(across)


def spread_grad(grad_out, wait):
    row, col = lax.axis_index("row"), lax.axis_index("col")
    breadth = grad_out.shape[1] // 2
    pieces = []
    for step in range(4):
        pairs = [
            (((2 * (r % 2) + c) ^ step) * 2 + r // 2, r * 2 + c) for r in range(4) for c in range(2)
        ]
        second = ((row ^ step) >> 1) & 1
        part = columns(grad_out, second * breadth, breadth)
        pieces.append(lax.ppermute(part, ("row", "col"), pairs))
    stacked = after(jnp.stack(pieces), wait)
    base = 2 * (row & 1) + col
    order = [row, row ^ 1, jnp.where(row < 2, 2, 1), jnp.where(row < 2, 3, 0)]
    return jnp.concatenate([pick(stacked, base ^ r) for r in order])


def spread_gelu(gelu, early, waits, late):
    row, col = lax.axis_index("row"), lax.axis_index("col")
    half = gelu.shape[0] // 2
    units = gelu.shape[1] // 2
    other = after(over_col(lax.dynamic_slice_in_dim(gelu, (1 - col) * half, half, 0)), *early)
    own = lax.dynamic_slice_in_dim(gelu, col * half, half, 0)
    here = (row >> 1) == col
    pieces = []
    for bits in (3, 2, 1, 0):
        source = jnp.where(here == (bits < 2), own, other)
        piece = columns(source, ((row ^ bits) & 1) * units, units)
        pieces.insert(0, over_row(piece, bits) if bits else piece)
    mine = after(jnp.concatenate(pieces), *waits)
    return jnp.concatenate([mine, after(over_col(mine), *late)])


def hidden_kernel(stash, scale, *outs):
    halves, slopes = outs[:2], outs[2:]
    blocks = scale.shape[1]
    width = stash.shape[1] // blocks
    for b in range(blocks):
        before = stash[:, b * width : (b + 1) * width].astype(jnp.float32) * scale[:, b : b + 1]
        square = before * before
        tangent = jnp.tanh(root_two_over_pi * (before + cubic_coef * square * before))
        rise = 0.5 * (1.0 + tangent)
        value = before * rise
        slope = rise + 0.5 * before * (1.0 - tangent * tangent) * root_two_over_pi * (
            1.0 + 3.0 * cubic_coef * square
        )
        half, place = divmod(b, blocks // 2)
        halves[half][:, place * width : (place + 1) * width] = value.astype(jnp.bfloat16)
        group, inside = divmod(b, blocks // 8)
        chunk, inside = divmod(inside, blocks // (8 * CHUNKS))
        place = group * (blocks // (8 * CHUNKS)) + inside
        slopes[chunk][:, place * width : (place + 1) * width] = slope


def inputs_kernel(stash, scale, out):
    blocks = scale.shape[1]
    width = stash.shape[1] // blocks
    for b in range(blocks):
        part = slice(b * width, (b + 1) * width)
        out[:, part] = (stash[:, part].astype(jnp.float32) * scale[:, b : b + 1]).astype(jnp.bfloat16)


def elementwise(kernel, shapes, *operands):
    return pl.pallas_call(
        kernel,
        out_shape=shapes,
        compiler_params=pltpu.CompilerParams(vmem_limit_bytes=40 * 2**20),
        cost_estimate=pl.CostEstimate(
            flops=20 * operands[0].size,
            bytes_accessed=8 * operands[0].size,
            transcendentals=operands[0].size,
        ),
    )(*operands)


def chunk_rows(array, chunk):
    cut = array.reshape((8, CHUNKS, array.shape[0] // (8 * CHUNKS)) + array.shape[1:])
    return lax.index_in_dim(cut, chunk, 1, keepdims=False).reshape((-1,) + array.shape[1:])


def per_device_fast(
    grad_out, input_stash, input_scale, hidden_stash, hidden_scale, first_weight, second_weight
):
    col = lax.axis_index("col")
    mid = is_mid()
    tokens, units = hidden_stash.shape
    half = tokens // 2
    piece = units // (8 * CHUNKS)

    struct = jax.ShapeDtypeStruct
    local = elementwise(
        hidden_kernel,
        [struct((tokens, units // 2), jnp.bfloat16)] * 2
        + [struct((tokens, units // CHUNKS), jnp.float32)] * CHUNKS,
        hidden_stash,
        jnp.transpose(hidden_scale),
    )
    hidden_own, slopes = local[:2], local[2:]
    inputs_own = elementwise(
        inputs_kernel,
        struct(input_stash.shape, jnp.bfloat16),
        input_stash,
        jnp.transpose(input_scale),
    )

    inputs_near, inputs_others, inputs_across = row_gather(inputs_own)
    grad_rows = spread_grad(after(grad_out, inputs_own), inputs_near)
    first_half = row_gather(hidden_own[0])
    share = grad_rows.shape[1] // 4
    weights = [chunk_rows(second_weight, chunk) for chunk in range(CHUNKS)]
    grad_own, grad_partner = grad_rows[:tokens], grad_rows[tokens : 2 * tokens]
    grad_near, grad_others = grad_rows[: 2 * tokens], grad_rows[2 * tokens :]

    def second_term(near, others, _):
        def partial(d):
            return dot(near, columns(grad_near, d * share, share), contract_first) + dot(
                others, columns(grad_others, d * share, share), contract_first
            )

        return partial

    takens, ends, acrosses, besides = [], [], [], []
    for chunk in range(CHUNKS):
        weight = weights[chunk]
        rows = after(grad_others, first_half[0]) if chunk else grad_others

        def others():
            return dot(rows, weight, contract_last)

        sent = narrow(others())
        if chunk:
            sent = after(sent, takens[-1], inputs_across)
        takens.append(row_ends_in(sent))
        end, across, beside = row_scatter(
            others,
            lambda: dot(grad_partner, weight, contract_last),
            lambda weight=weight: dot(grad_own, weight, contract_last),
            takens[-1],
        )
        ends.append(end)
        acrosses.append(across)
        besides.append(beside)

    parts = [second_term(*first_half)]
    arrived = [depth_start(parts[0])]
    third, fourth = inputs_others[:tokens], inputs_others[tokens:]
    by_row = [
        inputs_near[:tokens],
        inputs_near[tokens:],
        jnp.where(mid, fourth, third),
        jnp.where(mid, third, fourth),
    ]
    inputs = jnp.concatenate(
        [jnp.where(col == 0, r[:half], r[half:]) for r in by_row]
        + [jnp.where(col == 0, r[half:], r[:half]) for r in by_row]
    )
    second_half = row_gather(after(hidden_own[1], besides[0]))
    parts.append(second_term(*second_half))

    gelus, firsts = [], []

    def first_term(gelu_rows):
        return lambda d: dot(inputs, columns(gelu_rows, d * piece, piece), contract_first)

    for chunk in range(CHUNKS):
        total = ends[chunk]()
        if chunk:
            early, waits, late = (firsts[-1][2],), (second_half[2],), (firsts[-1][1],)
        else:
            total = after(total, arrived[0][2])
            early, waits, late = (), (second_half[0],), (arrived[0][1],)
        gelu_rows = spread_gelu(narrow(total * slopes[chunk]), early, waits, late)
        gelus.append(gelu_rows)
        firsts.append(depth_start(first_term(gelu_rows)))
    arrived.append(depth_start(parts[1]))

    gelu_rows = jnp.concatenate(
        [g[:, d * piece : (d + 1) * piece] for d in range(4) for g in gelus], axis=1
    )
    cut = after(gelu_rows, firsts[-1][0]).reshape(2, 4, half, units // 2)

    def input_term(bits):
        return dot(cut[:, bits].reshape(tokens, -1), first_weight, contract_last)

    input_sum = [
        after(over_row(narrow(input_term(bits)), bits), firsts[-1][2], arrived[1][2])
        for bits in (3, 2, 1)
    ]
    input_grad = narrow(input_term(0) + sum(wide(part) for part in input_sum))
    front, back = input_grad[:half], input_grad[half:]
    input_grad = jnp.concatenate(
        [jnp.where(col == 0, front, back), jnp.where(col == 0, back, front)]
    )

    second_grad = jnp.concatenate([narrow(depth_end(p, a)) for p, a in zip(parts, arrived)])
    first_grad = jnp.concatenate(
        [narrow(depth_end(first_term(g), a)) for g, a in zip(gelus, firsts)], axis=1
    )

    def bias(array):
        sums = jnp.sum(wide(array), axis=0).reshape(4, -1)
        return depth_end(lambda d: pick(sums, d), depth_start(lambda d: pick(sums, d)))

    return input_grad, first_grad, bias(gelu_rows), second_grad, bias(grad_rows)


def solution(mesh):
    placed = (
        P(("row", "depth"), "col"),
        P(("row", "depth"), "col"),
        P("col", ("row", "depth")),
        P(("row", "depth"), "col"),
        P("col", ("row", "depth")),
        P("col", "row"),
        P("col", "row"),
    )
    sizes = dict(mesh.shape)
    fast = sizes["row"] == 4 and sizes["col"] == 2 and sizes["depth"] == 4
    return jax.shard_map(
        per_device_fast if fast else per_device_general,
        mesh=mesh,
        in_specs=placed,
        out_specs=(
            P(("row", "depth"), "col"),
            P("col", ("row", "depth")),
            P(("row", "depth")),
            P("col", ("row", "depth")),
            P(("row", "depth")),
        ),
        check_vma=False,
    )
```

```python
import jax
import jax.numpy as jnp
from jax import lax
from jax.experimental import pallas as pl
from jax.experimental.pallas import tpu as pltpu
from jax.sharding import PartitionSpec as P

root_two_over_pi = 0.7978845608028654
cubic_coef = 0.044715
contract_last = (((1,), (1,)), ((), ()))
contract_first = (((0,), (0,)), ((), ()))


def dequantize(values, scales):
    height = values.shape[0]
    breadth = values.shape[1]
    block = breadth // scales.shape[0]
    blocks = values.astype(jnp.float32).reshape(height, breadth // block, block)
    return (blocks * jnp.transpose(scales)[:, :, None]).reshape(height, breadth)


def gelu_value(before):
    tangent = jnp.tanh(root_two_over_pi * (before + cubic_coef * before * before * before))
    return 0.5 * before * (1.0 + tangent)


def gelu_slope(before):
    tangent = jnp.tanh(root_two_over_pi * (before + cubic_coef * before * before * before))
    return 0.5 * (1.0 + tangent) + 0.5 * before * (1.0 - tangent * tangent) * root_two_over_pi * (
        1.0 + 3.0 * cubic_coef * before * before
    )


def per_device_general(
    grad_out, input_stash, input_scale, hidden_stash, hidden_scale, first_weight, second_weight
):
    full_grad = lax.all_gather(grad_out, "col", axis=1, tiled=True)
    grad_rows = lax.all_to_all(full_grad, "row", split_axis=1, concat_axis=0, tiled=True)
    hidden_part = lax.dot_general(
        grad_rows, second_weight, contract_last, preferred_element_type=jnp.float32
    ).astype(jnp.bfloat16)
    hidden_grad = lax.psum_scatter(hidden_part, "row", scatter_dimension=0, tiled=True).astype(
        jnp.float32
    )
    before_gelu = dequantize(hidden_stash, hidden_scale)
    hidden_own = gelu_value(before_gelu).astype(jnp.bfloat16)
    gelu_grad = (hidden_grad * gelu_slope(before_gelu)).astype(jnp.bfloat16)
    full_gelu = lax.all_gather(gelu_grad, "col", axis=1, tiled=True)
    gelu_rows = lax.all_to_all(full_gelu, "row", split_axis=1, concat_axis=0, tiled=True)
    input_part = lax.dot_general(
        gelu_rows, first_weight, contract_last, preferred_element_type=jnp.float32
    ).astype(jnp.bfloat16)
    input_grad = lax.psum_scatter(input_part, "row", scatter_dimension=0, tiled=True)
    inputs_own = dequantize(input_stash, input_scale).astype(jnp.bfloat16)
    inputs = lax.all_gather(inputs_own, "row", axis=0, tiled=True)
    hidden = lax.all_gather(hidden_own, "row", axis=0, tiled=True)
    first_term = lax.dot_general(
        inputs, gelu_rows, contract_first, preferred_element_type=jnp.float32
    )
    first_column = jnp.sum(gelu_rows.astype(jnp.float32), axis=0)
    second_term = lax.dot_general(
        hidden, grad_rows, contract_first, preferred_element_type=jnp.float32
    )
    second_column = jnp.sum(grad_rows.astype(jnp.float32), axis=0)
    first_grad = lax.psum_scatter(
        first_term.astype(jnp.bfloat16), "depth", scatter_dimension=1, tiled=True
    )
    first_bias = lax.psum_scatter(
        first_column.astype(jnp.bfloat16), "depth", scatter_dimension=0, tiled=True
    ).astype(jnp.float32)
    second_grad = lax.psum_scatter(
        second_term.astype(jnp.bfloat16), "depth", scatter_dimension=1, tiled=True
    )
    second_bias = lax.psum_scatter(
        second_column.astype(jnp.bfloat16), "depth", scatter_dimension=0, tiled=True
    ).astype(jnp.float32)
    return input_grad, first_grad, first_bias, second_grad, second_bias


CHUNKS = 2


def dot(left, right, dims):
    return lax.dot_general(left, right, dims, preferred_element_type=jnp.float32)


def narrow(value):
    return value.astype(jnp.bfloat16)


def wide(value):
    return value.astype(jnp.float32)


def pick(array, index):
    return lax.dynamic_index_in_dim(array, index, 0, keepdims=False)


def columns(array, start, size):
    return lax.dynamic_slice_in_dim(array, start, size, 1)


def over_depth(value, bits):
    return lax.ppermute(value, "depth", [(i, i ^ bits) for i in range(4)])


def over_row(value, bits):
    return lax.ppermute(value, "row", [(i, i ^ bits) for i in range(4)])


def over_col(value):
    return lax.ppermute(value, "col", [(0, 1), (1, 0)])


def row_ends_in(value):
    return lax.ppermute(value, "row", [(0, 1), (3, 2)])


def row_mids_swap(value):
    return lax.ppermute(value, "row", [(1, 2), (2, 1)])


def row_mids_out(value):
    return lax.ppermute(value, "row", [(1, 0), (2, 3)])


def is_mid():
    row = lax.axis_index("row")
    return (row == 1) | (row == 2)


def after(value, *others):
    return lax.optimization_barrier((value,) + others)[0]


def row_gather(value, *waits):
    near = jnp.concatenate([value, over_row(value, 1)])
    across = row_mids_swap(after(near, *waits))
    return near, jnp.where(is_mid(), across, row_mids_out(across)), across


def row_scatter(others, partner, own, taken):
    passed = narrow(others() + wide(taken))
    across = row_mids_swap(passed)
    size = across.shape[0] // 2
    beside = over_row(narrow(partner() + wide(across[size:])), 1)
    return (lambda: own() + wide(across[:size]) + wide(beside)), across, beside, passed


def depth_start(partial):
    depth = lax.axis_index("depth")
    far = over_depth(narrow(partial(depth ^ 3)), 1)
    near = over_depth(narrow(partial(depth ^ 1)), 1)
    sent = narrow(partial(depth ^ 2) + wide(far))
    return near, over_depth(sent, 2), sent


def depth_end(partial, arrived):
    near, across, _ = arrived
    return partial(lax.axis_index("depth")) + wide(near) + wide(across)


def spread_grad(grad_out, wait):
    row, col = lax.axis_index("row"), lax.axis_index("col")
    breadth = grad_out.shape[1] // 2
    pieces = []
    for step in range(4):
        pairs = [
            (((2 * (r % 2) + c) ^ step) * 2 + r // 2, r * 2 + c) for r in range(4) for c in range(2)
        ]
        second = ((row ^ step) >> 1) & 1
        part = columns(grad_out, second * breadth, breadth)
        pieces.append(lax.ppermute(part, ("row", "col"), pairs))
    stacked = after(jnp.stack(pieces), wait)
    base = 2 * (row & 1) + col
    order = [row, row ^ 1, jnp.where(row < 2, 2, 1), jnp.where(row < 2, 3, 0)]
    return jnp.concatenate([pick(stacked, base ^ r) for r in order])


def spread_gelu(gelu, early, waits, late):
    row, col = lax.axis_index("row"), lax.axis_index("col")
    half = gelu.shape[0] // 2
    units = gelu.shape[1] // 2
    other = after(over_col(lax.dynamic_slice_in_dim(gelu, (1 - col) * half, half, 0)), *early)
    own = lax.dynamic_slice_in_dim(gelu, col * half, half, 0)
    here = (row >> 1) == col
    pieces = []
    for bits in (3, 2, 1, 0):
        source = jnp.where(here == (bits < 2), own, other)
        piece = columns(source, ((row ^ bits) & 1) * units, units)
        pieces.insert(0, over_row(piece, bits) if bits else piece)
    mine = after(jnp.concatenate(pieces), *waits)
    return jnp.concatenate([mine, after(over_col(mine), *late)])


def hidden_kernel(stash, scale, *outs):
    halves, slopes = outs[:2], outs[2:]
    blocks = scale.shape[1]
    width = stash.shape[1] // blocks
    for b in range(blocks):
        before = stash[:, b * width : (b + 1) * width].astype(jnp.float32) * scale[:, b : b + 1]
        square = before * before
        tangent = jnp.tanh(root_two_over_pi * (before + cubic_coef * square * before))
        rise = 0.5 * (1.0 + tangent)
        value = before * rise
        slope = rise + 0.5 * before * (1.0 - tangent * tangent) * root_two_over_pi * (
            1.0 + 3.0 * cubic_coef * square
        )
        half, place = divmod(b, blocks // 2)
        halves[half][:, place * width : (place + 1) * width] = value.astype(jnp.bfloat16)
        group, inside = divmod(b, blocks // 8)
        chunk, inside = divmod(inside, blocks // (8 * CHUNKS))
        place = group * (blocks // (8 * CHUNKS)) + inside
        slopes[chunk][:, place * width : (place + 1) * width] = slope


def inputs_kernel(stash, scale, out):
    blocks = scale.shape[1]
    width = stash.shape[1] // blocks
    for b in range(blocks):
        part = slice(b * width, (b + 1) * width)
        out[:, part] = (stash[:, part].astype(jnp.float32) * scale[:, b : b + 1]).astype(jnp.bfloat16)


def elementwise(kernel, shapes, *operands):
    return pl.pallas_call(
        kernel,
        out_shape=shapes,
        compiler_params=pltpu.CompilerParams(vmem_limit_bytes=40 * 2**20),
        cost_estimate=pl.CostEstimate(
            flops=20 * operands[0].size,
            bytes_accessed=8 * operands[0].size,
            transcendentals=operands[0].size,
        ),
    )(*operands)


def chunk_rows(array, chunk):
    cut = array.reshape((8, CHUNKS, array.shape[0] // (8 * CHUNKS)) + array.shape[1:])
    return lax.index_in_dim(cut, chunk, 1, keepdims=False).reshape((-1,) + array.shape[1:])


def per_device_fast(
    grad_out, input_stash, input_scale, hidden_stash, hidden_scale, first_weight, second_weight
):
    col = lax.axis_index("col")
    mid = is_mid()
    tokens, units = hidden_stash.shape
    half = tokens // 2
    piece = units // (8 * CHUNKS)

    struct = jax.ShapeDtypeStruct
    local = elementwise(
        hidden_kernel,
        [struct((tokens, units // 2), jnp.bfloat16)] * 2
        + [struct((tokens, units // CHUNKS), jnp.float32)] * CHUNKS,
        hidden_stash,
        jnp.transpose(hidden_scale),
    )
    hidden_own, slopes = local[:2], local[2:]
    inputs_own = elementwise(
        inputs_kernel,
        struct(input_stash.shape, jnp.bfloat16),
        input_stash,
        jnp.transpose(input_scale),
    )

    inputs_near, inputs_others, inputs_across = row_gather(inputs_own)
    grad_rows = spread_grad(after(grad_out, inputs_own), inputs_near)
    first_half = row_gather(hidden_own[0])
    share = grad_rows.shape[1] // 4
    weight_rows = after(second_weight, hidden_own[0])
    weights = [chunk_rows(weight_rows, chunk) for chunk in range(CHUNKS)]
    grad_own, grad_partner = grad_rows[:tokens], grad_rows[tokens : 2 * tokens]
    grad_near, grad_others = grad_rows[: 2 * tokens], grad_rows[2 * tokens :]

    def second_term(near, others, _):
        def partial(d):
            return dot(near, columns(grad_near, d * share, share), contract_first) + dot(
                others, columns(grad_others, d * share, share), contract_first
            )

        return partial

    own_rows = after(grad_own, first_half[0])
    takens, ends, acrosses, besides = [], [], [], []
    for chunk in range(CHUNKS):
        weight = weights[chunk]
        rows = after(grad_others, first_half[0]) if chunk else grad_others

        def others():
            return dot(rows, weight, contract_last)

        sent = narrow(others())
        if chunk:
            sent = after(sent, takens[-1], inputs_across)
        takens.append(row_ends_in(sent))
        end, across, beside, passed = row_scatter(
            others,
            lambda: dot(grad_partner, weight, contract_last),
            lambda weight=weight: dot(own_rows, weight, contract_last),
            takens[-1],
        )
        ends.append(end)
        acrosses.append(across)
        besides.append(beside)

    parts = [second_term(*first_half)]
    arrived = [depth_start(parts[0])]
    third, fourth = inputs_others[:tokens], inputs_others[tokens:]
    by_row = [
        inputs_near[:tokens],
        inputs_near[tokens:],
        jnp.where(mid, fourth, third),
        jnp.where(mid, third, fourth),
    ]
    inputs = jnp.concatenate(
        [jnp.where(col == 0, r[:half], r[half:]) for r in by_row]
        + [jnp.where(col == 0, r[half:], r[:half]) for r in by_row]
    )
    second_half = row_gather(after(hidden_own[1], besides[0]))
    parts.append(second_term(*second_half))

    gelus, firsts = [], []

    def first_term(gelu_rows):
        return lambda d: dot(inputs, columns(gelu_rows, d * piece, piece), contract_first)

    for chunk in range(CHUNKS):
        total = ends[chunk]()
        if chunk:
            early, waits, late = (firsts[-1][2],), (second_half[2],), (firsts[-1][1],)
        else:
            total = after(total, arrived[0][2], passed)
            early, waits, late = (), (second_half[0],), (arrived[0][1],)
        gelu_rows = spread_gelu(narrow(total * slopes[chunk]), early, waits, late)
        gelus.append(gelu_rows)
        firsts.append(depth_start(first_term(gelu_rows)))
    arrived.append(depth_start(parts[1]))

    gelu_rows = jnp.concatenate(
        [g[:, d * piece : (d + 1) * piece] for d in range(4) for g in gelus], axis=1
    )
    cut = after(gelu_rows, firsts[-1][0], arrived[1][2]).reshape(2, 4, half, units // 2)

    def input_term(bits):
        return dot(cut[:, bits].reshape(tokens, -1), first_weight, contract_last)

    input_sum = [
        after(over_row(narrow(input_term(bits)), bits), firsts[-1][2], arrived[1][1])
        for bits in (3, 2, 1)
    ]
    input_grad = narrow(input_term(0) + sum(wide(part) for part in input_sum))
    front, back = input_grad[:half], input_grad[half:]
    input_grad = jnp.concatenate(
        [jnp.where(col == 0, front, back), jnp.where(col == 0, back, front)]
    )

    second_grad = jnp.concatenate([narrow(depth_end(p, a)) for p, a in zip(parts, arrived)])
    first_grad = jnp.concatenate(
        [narrow(depth_end(first_term(g), a)) for g, a in zip(gelus, firsts)], axis=1
    )

    def bias(array):
        sums = jnp.sum(wide(array), axis=0).reshape(4, -1)
        return depth_end(lambda d: pick(sums, d), depth_start(lambda d: pick(sums, d)))

    return input_grad, first_grad, bias(gelu_rows), second_grad, bias(after(grad_rows, acrosses[0]))


def solution(mesh):
    placed = (
        P(("row", "depth"), "col"),
        P(("row", "depth"), "col"),
        P("col", ("row", "depth")),
        P(("row", "depth"), "col"),
        P("col", ("row", "depth")),
        P("col", "row"),
        P("col", "row"),
    )
    sizes = dict(mesh.shape)
    fast = sizes["row"] == 4 and sizes["col"] == 2 and sizes["depth"] == 4
    return jax.shard_map(
        per_device_fast if fast else per_device_general,
        mesh=mesh,
        in_specs=placed,
        out_specs=(
            P(("row", "depth"), "col"),
            P("col", ("row", "depth")),
            P(("row", "depth")),
            P("col", ("row", "depth")),
            P(("row", "depth")),
        ),
        check_vma=False,
    )
```

```python
import jax
import jax.numpy as jnp
from jax import lax
from jax.experimental import pallas as pl
from jax.experimental.pallas import tpu as pltpu
from jax.sharding import PartitionSpec as P

root_two_over_pi = 0.7978845608028654
cubic_coef = 0.044715
contract_last = (((1,), (1,)), ((), ()))
contract_first = (((0,), (0,)), ((), ()))


def dequantize(values, scales):
    height = values.shape[0]
    breadth = values.shape[1]
    block = breadth // scales.shape[0]
    blocks = values.astype(jnp.float32).reshape(height, breadth // block, block)
    return (blocks * jnp.transpose(scales)[:, :, None]).reshape(height, breadth)


def gelu_value(before):
    tangent = jnp.tanh(root_two_over_pi * (before + cubic_coef * before * before * before))
    return 0.5 * before * (1.0 + tangent)


def gelu_slope(before):
    tangent = jnp.tanh(root_two_over_pi * (before + cubic_coef * before * before * before))
    return 0.5 * (1.0 + tangent) + 0.5 * before * (1.0 - tangent * tangent) * root_two_over_pi * (
        1.0 + 3.0 * cubic_coef * before * before
    )


def per_device_general(
    grad_out, input_stash, input_scale, hidden_stash, hidden_scale, first_weight, second_weight
):
    full_grad = lax.all_gather(grad_out, "col", axis=1, tiled=True)
    grad_rows = lax.all_to_all(full_grad, "row", split_axis=1, concat_axis=0, tiled=True)
    hidden_part = lax.dot_general(
        grad_rows, second_weight, contract_last, preferred_element_type=jnp.float32
    ).astype(jnp.bfloat16)
    hidden_grad = lax.psum_scatter(hidden_part, "row", scatter_dimension=0, tiled=True).astype(
        jnp.float32
    )
    before_gelu = dequantize(hidden_stash, hidden_scale)
    hidden_own = gelu_value(before_gelu).astype(jnp.bfloat16)
    gelu_grad = (hidden_grad * gelu_slope(before_gelu)).astype(jnp.bfloat16)
    full_gelu = lax.all_gather(gelu_grad, "col", axis=1, tiled=True)
    gelu_rows = lax.all_to_all(full_gelu, "row", split_axis=1, concat_axis=0, tiled=True)
    input_part = lax.dot_general(
        gelu_rows, first_weight, contract_last, preferred_element_type=jnp.float32
    ).astype(jnp.bfloat16)
    input_grad = lax.psum_scatter(input_part, "row", scatter_dimension=0, tiled=True)
    inputs_own = dequantize(input_stash, input_scale).astype(jnp.bfloat16)
    inputs = lax.all_gather(inputs_own, "row", axis=0, tiled=True)
    hidden = lax.all_gather(hidden_own, "row", axis=0, tiled=True)
    first_term = lax.dot_general(
        inputs, gelu_rows, contract_first, preferred_element_type=jnp.float32
    )
    first_column = jnp.sum(gelu_rows.astype(jnp.float32), axis=0)
    second_term = lax.dot_general(
        hidden, grad_rows, contract_first, preferred_element_type=jnp.float32
    )
    second_column = jnp.sum(grad_rows.astype(jnp.float32), axis=0)
    first_grad = lax.psum_scatter(
        first_term.astype(jnp.bfloat16), "depth", scatter_dimension=1, tiled=True
    )
    first_bias = lax.psum_scatter(
        first_column.astype(jnp.bfloat16), "depth", scatter_dimension=0, tiled=True
    ).astype(jnp.float32)
    second_grad = lax.psum_scatter(
        second_term.astype(jnp.bfloat16), "depth", scatter_dimension=1, tiled=True
    )
    second_bias = lax.psum_scatter(
        second_column.astype(jnp.bfloat16), "depth", scatter_dimension=0, tiled=True
    ).astype(jnp.float32)
    return input_grad, first_grad, first_bias, second_grad, second_bias


CHUNKS = 2


def dot(left, right, dims):
    return lax.dot_general(left, right, dims, preferred_element_type=jnp.float32)


def narrow(value):
    return value.astype(jnp.bfloat16)


def wide(value):
    return value.astype(jnp.float32)


def pick(array, index):
    return lax.dynamic_index_in_dim(array, index, 0, keepdims=False)


def columns(array, start, size):
    return lax.dynamic_slice_in_dim(array, start, size, 1)


def over_depth(value, bits):
    return lax.ppermute(value, "depth", [(i, i ^ bits) for i in range(4)])


def over_row(value, bits):
    return lax.ppermute(value, "row", [(i, i ^ bits) for i in range(4)])


def over_col(value):
    return lax.ppermute(value, "col", [(0, 1), (1, 0)])


def row_ends_in(value):
    return lax.ppermute(value, "row", [(0, 1), (3, 2)])


def row_mids_swap(value):
    return lax.ppermute(value, "row", [(1, 2), (2, 1)])


def row_mids_out(value):
    return lax.ppermute(value, "row", [(1, 0), (2, 3)])


def is_mid():
    row = lax.axis_index("row")
    return (row == 1) | (row == 2)


def after(value, *others):
    return lax.optimization_barrier((value,) + others)[0]


def row_gather(value, *waits):
    near = jnp.concatenate([value, over_row(value, 1)])
    across = row_mids_swap(after(near, *waits))
    return near, jnp.where(is_mid(), across, row_mids_out(across)), across


def row_scatter(others, partner, own, taken):
    passed = narrow(others() + wide(taken))
    across = row_mids_swap(passed)
    size = across.shape[0] // 2
    beside = over_row(narrow(partner() + wide(across[size:])), 1)
    return (lambda: own() + wide(across[:size]) + wide(beside)), across, beside, passed


def depth_start(partial):
    depth = lax.axis_index("depth")
    far = over_depth(narrow(partial(depth ^ 3)), 1)
    near = over_depth(narrow(partial(depth ^ 1)), 1)
    sent = narrow(partial(depth ^ 2) + wide(far))
    return near, over_depth(sent, 2), sent


def depth_end(partial, arrived):
    near, across, _ = arrived
    return partial(lax.axis_index("depth")) + wide(near) + wide(across)


def spread_grad(grad_out, wait):
    row, col = lax.axis_index("row"), lax.axis_index("col")
    breadth = grad_out.shape[1] // 2
    pieces = []
    for step in range(4):
        pairs = [
            (((2 * (r % 2) + c) ^ step) * 2 + r // 2, r * 2 + c) for r in range(4) for c in range(2)
        ]
        second = ((row ^ step) >> 1) & 1
        part = columns(grad_out, second * breadth, breadth)
        pieces.append(lax.ppermute(part, ("row", "col"), pairs))
    stacked = after(jnp.stack(pieces), wait)
    base = 2 * (row & 1) + col
    order = [row, row ^ 1, jnp.where(row < 2, 2, 1), jnp.where(row < 2, 3, 0)]
    return jnp.concatenate([pick(stacked, base ^ r) for r in order])


def spread_gelu(gelu, early, waits, late):
    row, col = lax.axis_index("row"), lax.axis_index("col")
    half = gelu.shape[0] // 2
    units = gelu.shape[1] // 2
    other = after(over_col(lax.dynamic_slice_in_dim(gelu, (1 - col) * half, half, 0)), *early)
    own = lax.dynamic_slice_in_dim(gelu, col * half, half, 0)
    here = (row >> 1) == col
    pieces = []
    for bits in (3, 2, 1, 0):
        source = jnp.where(here == (bits < 2), own, other)
        piece = columns(source, ((row ^ bits) & 1) * units, units)
        pieces.insert(0, over_row(piece, bits) if bits else piece)
    mine = after(jnp.concatenate(pieces), *waits)
    return jnp.concatenate([mine, after(over_col(mine), *late)])


def hidden_kernel(stash, scale, *outs):
    halves, slopes = outs[:2], outs[2:]
    blocks = scale.shape[1]
    width = stash.shape[1] // blocks
    for b in range(blocks):
        before = stash[:, b * width : (b + 1) * width].astype(jnp.float32) * scale[:, b : b + 1]
        square = before * before
        tangent = jnp.tanh(root_two_over_pi * (before + cubic_coef * square * before))
        rise = 0.5 * (1.0 + tangent)
        value = before * rise
        slope = rise + 0.5 * before * (1.0 - tangent * tangent) * root_two_over_pi * (
            1.0 + 3.0 * cubic_coef * square
        )
        half, place = divmod(b, blocks // 2)
        halves[half][:, place * width : (place + 1) * width] = value.astype(jnp.bfloat16)
        group, inside = divmod(b, blocks // 8)
        chunk, inside = divmod(inside, blocks // (8 * CHUNKS))
        place = group * (blocks // (8 * CHUNKS)) + inside
        slopes[chunk][:, place * width : (place + 1) * width] = slope


def inputs_kernel(stash, scale, out):
    blocks = scale.shape[1]
    width = stash.shape[1] // blocks
    for b in range(blocks):
        part = slice(b * width, (b + 1) * width)
        out[:, part] = (stash[:, part].astype(jnp.float32) * scale[:, b : b + 1]).astype(jnp.bfloat16)


def elementwise(kernel, shapes, *operands):
    return pl.pallas_call(
        kernel,
        out_shape=shapes,
        compiler_params=pltpu.CompilerParams(vmem_limit_bytes=40 * 2**20),
        cost_estimate=pl.CostEstimate(
            flops=20 * operands[0].size,
            bytes_accessed=8 * operands[0].size,
            transcendentals=operands[0].size,
        ),
    )(*operands)


def chunk_rows(array, chunk):
    cut = array.reshape((8, CHUNKS, array.shape[0] // (8 * CHUNKS)) + array.shape[1:])
    return lax.index_in_dim(cut, chunk, 1, keepdims=False).reshape((-1,) + array.shape[1:])


def per_device_fast(
    grad_out, input_stash, input_scale, hidden_stash, hidden_scale, first_weight, second_weight
):
    col = lax.axis_index("col")
    mid = is_mid()
    tokens, units = hidden_stash.shape
    half = tokens // 2
    piece = units // (8 * CHUNKS)

    struct = jax.ShapeDtypeStruct
    local = elementwise(
        hidden_kernel,
        [struct((tokens, units // 2), jnp.bfloat16)] * 2
        + [struct((tokens, units // CHUNKS), jnp.float32)] * CHUNKS,
        hidden_stash,
        jnp.transpose(hidden_scale),
    )
    hidden_own, slopes = local[:2], local[2:]
    inputs_own = elementwise(
        inputs_kernel,
        struct(input_stash.shape, jnp.bfloat16),
        input_stash,
        jnp.transpose(input_scale),
    )

    inputs_near, inputs_others, inputs_across = row_gather(inputs_own)
    grad_rows = spread_grad(after(grad_out, inputs_own), inputs_near)
    first_half = row_gather(hidden_own[0])
    share = grad_rows.shape[1] // 4
    weight_rows = after(second_weight, hidden_own[0])
    weights = [chunk_rows(weight_rows, chunk) for chunk in range(CHUNKS)]
    grad_own, grad_partner = grad_rows[:tokens], grad_rows[tokens : 2 * tokens]
    grad_near, grad_others = grad_rows[: 2 * tokens], grad_rows[2 * tokens :]

    def second_term(near, others, _):
        def partial(d):
            return dot(near, columns(grad_near, d * share, share), contract_first) + dot(
                others, columns(grad_others, d * share, share), contract_first
            )

        return partial

    own_rows = after(grad_own, first_half[0])
    takens, ends, acrosses, besides = [], [], [], []
    for chunk in range(CHUNKS):
        weight = weights[chunk]
        rows = after(grad_others, first_half[0]) if chunk else grad_others

        def others():
            return dot(rows, weight, contract_last)

        sent = narrow(others())
        if chunk:
            sent = after(sent, takens[-1], inputs_across)
        takens.append(row_ends_in(sent))
        end, across, beside, passed = row_scatter(
            others,
            lambda: dot(grad_partner, weight, contract_last),
            lambda weight=weight: dot(own_rows, weight, contract_last),
            takens[-1],
        )
        ends.append(end)
        acrosses.append(across)
        besides.append(beside)

    parts = [second_term(*first_half)]
    arrived = [depth_start(parts[0])]
    third, fourth = inputs_others[:tokens], inputs_others[tokens:]
    by_row = [
        inputs_near[:tokens],
        inputs_near[tokens:],
        jnp.where(mid, fourth, third),
        jnp.where(mid, third, fourth),
    ]
    inputs = jnp.concatenate(
        [jnp.where(col == 0, r[:half], r[half:]) for r in by_row]
        + [jnp.where(col == 0, r[half:], r[:half]) for r in by_row]
    )
    second_half = row_gather(after(hidden_own[1], acrosses[0]))
    parts.append(second_term(*second_half))

    gelus, firsts = [], []

    def first_term(gelu_rows):
        return lambda d: dot(inputs, columns(gelu_rows, d * piece, piece), contract_first)

    for chunk in range(CHUNKS):
        total = ends[chunk]()
        if chunk:
            early, waits, late = (firsts[-1][2],), (second_half[2],), (firsts[-1][1],)
        else:
            total = after(total, arrived[0][2], passed)
            early, waits, late = (), (second_half[0],), (arrived[0][1],)
        gelu_rows = spread_gelu(narrow(total * slopes[chunk]), early, waits, late)
        gelus.append(gelu_rows)
        firsts.append(depth_start(first_term(gelu_rows)))
    arrived.append(depth_start(parts[1]))

    gelu_rows = jnp.concatenate(
        [g[:, d * piece : (d + 1) * piece] for d in range(4) for g in gelus], axis=1
    )
    cut = after(gelu_rows, firsts[-1][0], arrived[1][2]).reshape(2, 4, half, units // 2)

    def input_term(bits):
        return dot(cut[:, bits].reshape(tokens, -1), first_weight, contract_last)

    input_sum = [
        after(over_row(narrow(input_term(bits)), bits), firsts[-1][2], arrived[1][1])
        for bits in (3, 2, 1)
    ]
    input_grad = narrow(input_term(0) + sum(wide(part) for part in input_sum))
    front, back = input_grad[:half], input_grad[half:]
    input_grad = jnp.concatenate(
        [jnp.where(col == 0, front, back), jnp.where(col == 0, back, front)]
    )

    second_grad = jnp.concatenate([narrow(depth_end(p, a)) for p, a in zip(parts, arrived)])
    first_grad = jnp.concatenate(
        [narrow(depth_end(first_term(g), a)) for g, a in zip(gelus, firsts)], axis=1
    )

    def bias(array):
        sums = jnp.sum(wide(array), axis=0).reshape(4, -1)
        return depth_end(lambda d: pick(sums, d), depth_start(lambda d: pick(sums, d)))

    return input_grad, first_grad, bias(gelu_rows), second_grad, bias(after(grad_rows, acrosses[0]))


def solution(mesh):
    placed = (
        P(("row", "depth"), "col"),
        P(("row", "depth"), "col"),
        P("col", ("row", "depth")),
        P(("row", "depth"), "col"),
        P("col", ("row", "depth")),
        P("col", "row"),
        P("col", "row"),
    )
    sizes = dict(mesh.shape)
    fast = sizes["row"] == 4 and sizes["col"] == 2 and sizes["depth"] == 4
    return jax.shard_map(
        per_device_fast if fast else per_device_general,
        mesh=mesh,
        in_specs=placed,
        out_specs=(
            P(("row", "depth"), "col"),
            P("col", ("row", "depth")),
            P(("row", "depth")),
            P("col", ("row", "depth")),
            P(("row", "depth")),
        ),
        check_vma=False,
    )
```
